32 devices in a mesh: path: 16 (over z, y, x), mod: 2 (over core).
Axes of the slice: x: 2, y: 2, z: 4, core: 2. Of those that a mesh axis runs over, the one named last changes fastest.
Arguments:
- tokens: bfloat16 [16, 384, 3072], P('path', None, 'mod'), may hold values from -48 to 48
- cotangent: bfloat16 [16, 384, 3072], P('path', None, 'mod'), may hold values from -1.5 to 1.5
- path_modules: int32 [16, 1], replicated, may hold values from 0 to 7, as said below
- path_in: bfloat16 [16, 1, 3072, 1024], P('path', None, 'mod'), may hold values from -0.109375 to 0.109375
- path_out: bfloat16 [16, 1, 3072, 1024], P('path', None, 'mod'), may hold values from -0.1875 to 0.1875
- outer_in: float32 [1, 8, 3072, 1024], P(None, None, ('mod', 'path')), may hold values from -0.109375 to 0.109375
- outer_out: float32 [1, 8, 3072, 1024], P(None, None, ('mod', 'path')), may hold values from -0.1875 to 0.1875
- moment_in: float32 [1, 8, 3072, 1024], P(None, None, ('mod', 'path')), may hold values from -0.125 to 0.125
- moment_out: float32 [1, 8, 3072, 1024], P(None, None, ('mod', 'path')), may hold values from -0.4375 to 0.4375
Outputs:
- block_out: bfloat16 [16, 384, 3072], P('path', None, 'mod')
- grad_in: bfloat16 [16, 1, 3072, 1024], P('path', None, 'mod')
- grad_out: bfloat16 [16, 1, 3072, 1024], P('path', None, 'mod')
The draws below stay inside these ranges and needn't reach their ends.
Inputs may be any that keep to these rules, and one draw needn't show every extreme that they name: `path_modules`: every module of each level is read by at least one path.
All inputs are finite; a program needn't handle non-finite values.
Results may differ from the reference program's by a relative error of at most 0.0071.
Values may be sent and summed in bfloat16 or wider, within the bound.
A program may use at most 128 MiB of HBM per device.

```python
import jax
import jax.numpy as jnp
from jax import lax

D = 3072
EH = 1024
MODS = 8
LEVELS = 1
TOK = 384
PATHS = 16


def draw_tokens(key, part):
    first, second, third = jax.random.split(key, 3)
    column = jnp.arange(D, dtype=jnp.float32) / D
    base = jnp.clip(jax.random.normal(first, (PATHS, TOK, D), jnp.float32), -6.0, 6.0)
    profile = jnp.power(10.0, 0.5 * column - 0.25)
    rough = jax.random.uniform(second, (D,), jnp.float32, 0.7, 1.3)
    rows_scale = jnp.power(10.0, jax.random.uniform(third, (PATHS, TOK, 1), jnp.float32, -0.5, 0.5))
    return (base * profile * rough * rows_scale).astype(jnp.bfloat16)


def draw_path_modules(key, part):
    columns = []
    for level in range(LEVELS):
        level_key = jax.random.fold_in(key, level + 11)
        first, second, third, fourth = jax.random.split(level_key, 4)
        draw_one = jax.random.randint(first, (PATHS,), 0, MODS)
        draw_two = jax.random.randint(second, (PATHS,), 0, MODS)
        picked = jnp.minimum(draw_one, draw_two)
        places = jax.random.permutation(third, PATHS)[:MODS]
        picked = picked.at[places].set(jnp.arange(MODS, dtype=jnp.int32))
        relabel = jax.random.permutation(fourth, MODS)
        columns.append(relabel[picked])
    return jnp.stack(columns, axis=1).astype(jnp.int32)


def shard_levels(key, extent, pieces, low, top_value):
    def one(position, parts):
        heights = jax.random.uniform(jax.random.fold_in(jax.random.fold_in(key, 6), position), (parts,), jnp.float32, low / len(pieces), top_value / len(pieces))
        return jnp.repeat(jnp.exp(heights), extent[position] // parts).reshape((-1,) + (1,) * (len(extent) - position - 1))

    gain = one(*pieces[0])
    for cut in pieces[1:]:
        gain = gain * one(*cut)
    return gain


def scatter_about(stream_key, dims, scale, limit, cuts=(), kind=jnp.bfloat16):
    drawn = jax.random.normal(stream_key, dims, jnp.float32) * scale
    if len(cuts) > 0:
        drawn = shard_levels(stream_key, dims, cuts, -0.22, 0.18) * drawn
    return jnp.clip(drawn, min=-limit, max=limit).astype(kind)


def setup_inputs(seed: int = 0) -> dict:
    streams_of = jax.random.split(jax.random.key(seed), 10)
    return {
        "tokens": draw_tokens(jax.random.fold_in(streams_of[9], 71), 0),
        "cotangent": scatter_about(streams_of[1], (PATHS, TOK, D), 0.1, 1.5, ((0, 16), (2, 2))),
        "path_modules": draw_path_modules(jax.random.fold_in(streams_of[9], 71), 0),
        "path_in": scatter_about(streams_of[3], (PATHS, LEVELS, D, EH), D ** -0.5, 0.109375, ((0, 16), (2, 2))),
        "path_out": scatter_about(streams_of[4], (PATHS, LEVELS, D, EH), EH ** -0.5, 0.1875, ((0, 16), (2, 2))),
        "outer_in": scatter_about(streams_of[5], (LEVELS, MODS, D, EH), D ** -0.5, 0.109375, ((2, 32),), jnp.float32),
        "outer_out": scatter_about(streams_of[6], (LEVELS, MODS, D, EH), EH ** -0.5, 0.1875, ((2, 32),), jnp.float32),
        "moment_in": scatter_about(streams_of[7], (LEVELS, MODS, D, EH), 0.008, 0.125, ((2, 32),), jnp.float32),
        "moment_out": scatter_about(streams_of[8], (LEVELS, MODS, D, EH), 0.03, 0.4375, ((2, 32),), jnp.float32),
    }


epsilon = 1e-05
outer_rate = 0.7
outer_momentum = 0.9

def outer_step(outer, moment, average):
    delta = outer - average
    moment_next = outer_momentum * moment + delta
    return (outer - outer_rate * (delta + outer_momentum * moment_next)).astype(jnp.bfloat16)

def silu_slope(pre):
    sigmoid_z = jax.nn.sigmoid(pre)
    return sigmoid_z * (1.0 + pre * (1.0 - sigmoid_z))

def path_pass(inputs, upstream, weight_in, weight_out):
    state = inputs
    saved = []
    for level in range(LEVELS):
        wide = state.astype(jnp.float32)
        scale = lax.rsqrt(lax.optimization_barrier(jnp.sum(wide * wide, axis=1)) / D + epsilon)[:, None]
        normal = wide * scale
        normed = normal.astype(jnp.bfloat16)
        pre = jnp.dot(normed, weight_in[level], preferred_element_type=jnp.float32)
        act = jax.nn.silu(pre).astype(jnp.bfloat16)
        branch = lax.dot_general(act, weight_out[level], (((1,), (1,)), ((), ())), preferred_element_type=jnp.float32)
        saved.append((scale, normal, normed, pre, act))
        state = (wide + branch).astype(jnp.bfloat16)
    grads_in = [None] * LEVELS
    grads_out = [None] * LEVELS
    for level in reversed(range(LEVELS)):
        scale, normal, normed, pre, act = saved[level]
        grads_out[level] = lax.dot_general(upstream, act, (((0,), (0,)), ((), ())), preferred_element_type=jnp.float32).astype(jnp.bfloat16)
        slope = jnp.dot(upstream, weight_out[level], preferred_element_type=jnp.float32)
        pregrad = (slope * silu_slope(pre)).astype(jnp.bfloat16)
        grads_in[level] = lax.dot_general(normed, pregrad, (((0,), (0,)), ((), ())), preferred_element_type=jnp.float32).astype(jnp.bfloat16)
        if level > 0:
            normgrad = lax.dot_general(pregrad, weight_in[level], (((1,), (1,)), ((), ())), preferred_element_type=jnp.float32)
            inner = (lax.optimization_barrier(jnp.sum(normgrad * normal, axis=1)) / D)[:, None]
            upstream = (upstream.astype(jnp.float32) + scale * (normgrad - normal * inner)).astype(jnp.bfloat16)
    return (state, jnp.stack(grads_in), jnp.stack(grads_out))

def reference(tokens, cotangent, path_modules, path_in, path_out, outer_in, outer_out, moment_in, moment_out):
    picked_in = []
    picked_out = []
    for level in range(LEVELS):
        chosen = path_modules[:, level]
        member = chosen[None, :] == jnp.arange(MODS, dtype=jnp.int32)[:, None]
        counts = lax.optimization_barrier(jnp.sum(member.astype(jnp.float32), axis=1))[:, None, None]
        member_bf = member.astype(jnp.bfloat16)
        summed_in = jnp.dot(member_bf, path_in[:, level].reshape(PATHS, D * EH), preferred_element_type=jnp.float32)
        summed_out = jnp.dot(member_bf, path_out[:, level].reshape(PATHS, D * EH), preferred_element_type=jnp.float32)
        fresh_in = outer_step(outer_in[level], moment_in[level], summed_in.reshape(MODS, D, EH) / counts)
        fresh_out = outer_step(outer_out[level], moment_out[level], summed_out.reshape(MODS, D, EH) / counts)
        picked_in.append(jnp.take(fresh_in, chosen, axis=0))
        picked_out.append(jnp.take(fresh_out, chosen, axis=0))
    weight_in = jnp.stack(picked_in, axis=1)
    weight_out = jnp.stack(picked_out, axis=1)

    def one_path(items):
        return path_pass(items[0], items[1], items[2], items[3])
    block_out, grad_in, grad_out = lax.map(one_path, (tokens, cotangent, weight_in, weight_out))
    return (block_out, grad_in, grad_out)
```

```python
import functools

import jax
import jax.numpy as jnp
from jax import lax
from jax.experimental import pallas as pl
from jax.experimental.pallas import tpu as pltpu
from jax.sharding import PartitionSpec as P

D = 3072


epsilon = 1e-05
outer_rate = 0.7
outer_momentum = 0.9


def outer_step(outer, moment, average):
    delta = outer - average
    moment_next = outer_momentum * moment + delta
    return (outer - outer_rate * (delta + outer_momentum * moment_next)).astype(jnp.bfloat16)


def silu_slope(pre):
    sigmoid_z = jax.nn.sigmoid(pre)
    return sigmoid_z * (1.0 + pre * (1.0 - sigmoid_z))


def token_total(values):
    return lax.psum(values, "mod")


def share_total(left, right):
    return lax.psum_scatter(
        jnp.dot(left, right, preferred_element_type=jnp.float32),
        "mod",
        scatter_dimension=0,
        tiled=True,
    )


def share_gather(values):
    return lax.all_gather(values, "mod", axis=0, tiled=True)


def hidden_forward(normed, weight_level):
    pre_share = share_total(normed, weight_level)
    act_share = jax.nn.silu(pre_share).astype(jnp.bfloat16)
    return (pre_share, share_gather(act_share))


def hidden_backward(upstream, weight_level, pre):
    slope_share = share_total(upstream, weight_level)
    return share_gather((slope_share * silu_slope(pre)).astype(jnp.bfloat16))


def local(
    tokens, cotangent, path_modules, path_in, path_out, outer_in, outer_out, moment_in, moment_out
):
    path_count = lax.axis_size("path")
    level_count = path_in.shape[1]
    local_rows = path_in.shape[2]
    hidden = path_in.shape[3]
    module_count = outer_in.shape[1]
    owner_rows = outer_in.shape[2]
    piece_shape = (level_count, path_count, owner_rows, hidden)
    arrived_in, arrived_out = (
        lax.all_to_all(
            path_in.reshape(piece_shape), "path", split_axis=1, concat_axis=1, tiled=True
        ),
        lax.all_to_all(
            path_out.reshape(piece_shape), "path", split_axis=1, concat_axis=1, tiled=True
        ),
    )
    level = 0
    chosen = path_modules[:, level]
    member = chosen[None, :] == jnp.arange(module_count, dtype=jnp.int32)[:, None]
    counts = jnp.sum(member.astype(jnp.float32), axis=1)[:, None, None]
    member_bf = member.astype(jnp.bfloat16)
    summed_in = jnp.dot(
        member_bf,
        arrived_in[level].reshape(path_count, owner_rows * hidden),
        preferred_element_type=jnp.float32,
    )
    summed_out = jnp.dot(
        member_bf,
        arrived_out[level].reshape(path_count, owner_rows * hidden),
        preferred_element_type=jnp.float32,
    )
    fresh_in = outer_step(
        outer_in[level],
        moment_in[level],
        summed_in.reshape(module_count, owner_rows, hidden) / counts,
    )
    fresh_out = outer_step(
        outer_out[level],
        moment_out[level],
        summed_out.reshape(module_count, owner_rows, hidden) / counts,
    )
    picked_in = jnp.stack([jnp.take(fresh_in, path_modules[:, 0], axis=0)])
    picked_out = jnp.stack([jnp.take(fresh_out, path_modules[:, 0], axis=0)])
    back_in, back_out = (
        lax.all_to_all(picked_in, "path", split_axis=1, concat_axis=1, tiled=True),
        lax.all_to_all(picked_out, "path", split_axis=1, concat_axis=1, tiled=True),
    )
    weight_in = back_in.reshape(level_count, local_rows, hidden)
    weight_out = back_out.reshape(level_count, local_rows, hidden)
    state = tokens[0]
    level = 0
    wide = state.astype(jnp.float32)
    scale = lax.rsqrt(token_total(jnp.sum(wide * wide, axis=1)) / D + epsilon)[:, None]
    normal = wide * scale
    normed = normal.astype(jnp.bfloat16)
    pre, act = hidden_forward(normed, weight_in[level])
    branch = lax.dot_general(
        act, weight_out[level], (((1,), (1,)), ((), ())), preferred_element_type=jnp.float32
    )
    saved = [(scale, normal, normed, pre, act)]
    state = (wide + branch).astype(jnp.bfloat16)
    upstream = cotangent[0]
    grads_in = [None] * level_count
    grads_out = [None] * level_count
    for level in reversed(range(level_count)):
        scale, normal, normed, pre, act = saved[level]
        grads_out[level] = lax.dot_general(
            upstream, act, (((0,), (0,)), ((), ())), preferred_element_type=jnp.float32
        ).astype(jnp.bfloat16)
        pregrad = hidden_backward(upstream, weight_out[level], pre)
        grads_in[level] = lax.dot_general(
            normed, pregrad, (((0,), (0,)), ((), ())), preferred_element_type=jnp.float32
        ).astype(jnp.bfloat16)
    return (state[None], jnp.stack(grads_in)[None], jnp.stack(grads_out)[None])


MESH = pl.DeviceIdType.MESH
F32 = jnp.float32
BF16 = jnp.bfloat16
TILE = 256


def far_first(count):
    return sorted(range(1, count), key=lambda step: (abs(2 * step - count), step))


def fused_kernel(
    dims,
    pm_ref,
    tok_hbm,
    cot_hbm,
    path_in,
    path_out,
    outer_in,
    outer_out,
    moment_in,
    moment_out,
    block_hbm,
    gin_hbm,
    gout_hbm,
    arr_in,
    arr_out,
    outer_v,
    moment_v,
    fresh,
    pick_in,
    pick_out,
    w_in,
    w_out,
    tok,
    cot,
    normed,
    norm_mine,
    norm_other,
    pre_mine,
    pre_other,
    slope_mine,
    slope_other,
    act,
    pregrad,
    gin_v,
    gout_v,
    state_v,
    member,
    count,
    send_sems,
    recv_sems,
    own_sems,
    pair_send,
    pair_recv,
    load_sems,
    out_sems,
):
    paths, modules, rows, owner, hidden, tokens, width = dims
    me = lax.axis_index("path")
    core = lax.axis_index("mod")
    steps = far_first(paths)
    tiles = hidden // TILE

    barrier = pltpu.get_barrier_semaphore()
    for step in steps:
        pl.semaphore_signal(
            barrier, inc=1, device_id=(lax.rem(me + step, paths), core), device_id_type=MESH
        )
    pl.semaphore_signal(barrier, inc=1, device_id=(me, 1 - core), device_id_type=MESH)
    pl.semaphore_wait(barrier, paths)

    def span(index):
        return pl.ds(pl.multiple_of(index * owner, 16), owner)

    def gather_copy(kind, step, whole, arrived):
        dest = lax.rem(me + step, paths)
        return pltpu.make_async_remote_copy(
            src_ref=whole.at[span(dest)],
            dst_ref=arrived.at[me],
            send_sem=send_sems.at[kind, step],
            recv_sem=recv_sems.at[kind, step],
            device_id=(dest, core),
            device_id_type=MESH,
        )

    def spread_copy(kind, step, picked, weight):
        dest = lax.rem(me + step, paths)
        return pltpu.make_async_remote_copy(
            src_ref=picked.at[dest],
            dst_ref=weight.at[span(me)],
            send_sem=send_sems.at[kind, step],
            recv_sem=recv_sems.at[kind, step],
            device_id=(dest, core),
            device_id_type=MESH,
        )

    def pair_copy(slot, source, target):
        return pltpu.make_async_remote_copy(
            src_ref=source,
            dst_ref=target,
            send_sem=pair_send.at[slot],
            recv_sem=pair_recv.at[slot],
            device_id=(me, 1 - core),
            device_id_type=MESH,
        )

    for step in steps:
        gather_copy(0, step, path_in, arr_in).start()
    for step in steps:
        gather_copy(1, step, path_out, arr_out).start()

    own_in = pltpu.make_async_copy(path_in.at[span(me)], arr_in.at[me], own_sems.at[0])
    own_out = pltpu.make_async_copy(path_out.at[span(me)], arr_out.at[me], own_sems.at[1])
    load_tok = pltpu.make_async_copy(tok_hbm, tok, load_sems.at[0])
    load_cot = pltpu.make_async_copy(cot_hbm, cot, load_sems.at[1])
    load_outer = pltpu.make_async_copy(outer_in, outer_v, load_sems.at[2])
    load_moment = pltpu.make_async_copy(moment_in, moment_v, load_sems.at[3])
    for copy in (load_tok, load_cot, own_in, own_out, load_outer, load_moment):
        copy.start()

    for k in range(modules):
        total = jnp.float32(0.0)
        for p in range(paths):
            flag = jnp.where(pm_ref[p, 0] == k, jnp.float32(1.0), jnp.float32(0.0))
            member[k * paths + p] = flag
            total = total + flag
        count[k] = total

    load_tok.wait()
    block = 32

    @pl.loop(0, tokens // block)
    def _(i):
        at = pl.ds(pl.multiple_of(i * block, block), block)
        wide = tok[at, :].astype(F32)
        norm_mine[at, :] = jnp.broadcast_to(
            jnp.sum(wide * wide, axis=1, keepdims=True), (block, 128)
        )

    pair = pair_copy(0, norm_mine, norm_other)
    pair.start()
    pair.wait()

    @pl.loop(0, tokens // block)
    def _(i):
        at = pl.ds(pl.multiple_of(i * block, block), block)
        total = norm_mine[at, :][:, :1] + norm_other[at, :][:, :1]
        scale = lax.rsqrt(total / width + epsilon)
        normed[at, :] = (tok[at, :].astype(F32) * scale).astype(BF16)

    load_cot.wait()

    def update(arrived):
        columns = hidden // TILE

        @pl.loop(0, (owner // 16) * columns)
        def _(i):
            at = pl.ds(pl.multiple_of((i // columns) * 16, 16), 16)
            col = pl.ds(pl.multiple_of((i % columns) * TILE, TILE), TILE)
            sums = [jnp.zeros((16, TILE), F32) for _ in range(modules)]
            for p in range(paths):
                x = arrived[p, at, col].astype(F32)
                for k in range(modules):
                    sums[k] = sums[k] + member[k * paths + p] * x
            for k in range(modules):
                average = sums[k] / count[k]
                fresh[k, at, col] = outer_step(
                    outer_v[k, at, col], moment_v[k, at, col], average
                )

    def spread(kind, picked, weight):
        for step in steps:
            dest = lax.rem(me + step, paths)
            picked[dest] = fresh[pm_ref[dest, 0]]
            spread_copy(kind, step, picked, weight).start()
        weight[span(me), :] = fresh[pm_ref[me, 0]]

    own_in.wait()
    load_outer.wait()
    load_moment.wait()
    for step in steps:
        gather_copy(0, step, path_in, arr_in).wait_recv()
    update(arr_in)
    load_outer = pltpu.make_async_copy(outer_out, outer_v, load_sems.at[2])
    load_moment = pltpu.make_async_copy(moment_out, moment_v, load_sems.at[3])
    load_outer.start()
    load_moment.start()
    spread(2, pick_in, w_in)

    own_out.wait()
    load_outer.wait()
    load_moment.wait()
    for step in steps:
        gather_copy(1, step, path_out, arr_out).wait_recv()
    update(arr_out)
    spread(3, pick_out, w_out)

    for step in steps:
        spread_copy(2, step, pick_in, w_in).wait_recv()

    @pl.loop(0, tiles)
    def _(j):
        col = pl.ds(pl.multiple_of(j * TILE, TILE), TILE)
        pre_mine[j] = jnp.dot(normed[...], w_in[:, col], preferred_element_type=F32)

    pair = pair_copy(1, pre_mine, pre_other)
    pair.start()
    pair.wait()

    for j in range(tiles):

        @pl.loop(0, tokens // block)
        def _(i):
            at = pl.ds(pl.multiple_of(i * block, block), block)
            pre = pre_mine[j, at, :] + pre_other[j, at, :]
            sigmoid = jax.nn.sigmoid(pre)
            act[at, j * TILE : (j + 1) * TILE] = (pre * sigmoid).astype(BF16)
            pre_mine[j, at, :] = sigmoid * (1.0 + pre * (1.0 - sigmoid))

    @pl.loop(0, tiles)
    def _(j):
        col = pl.ds(pl.multiple_of(j * TILE, TILE), TILE)
        gout_v[:, col] = lax.dot_general(
            cot[...], act[:, col], (((0,), (0,)), ((), ())), preferred_element_type=F32
        ).astype(BF16)

    store_gout = pltpu.make_async_copy(gout_v, gout_hbm, out_sems.at[0])
    store_gout.start()

    for step in steps:
        spread_copy(3, step, pick_out, w_out).wait_recv()

    pairs = []
    for j in range(tiles):
        slope_mine[j] = jnp.dot(
            cot[...], w_out[:, j * TILE : (j + 1) * TILE], preferred_element_type=F32
        )
        pairs.append(pair_copy(2 + j, slope_mine.at[j], slope_other.at[j]))
        pairs[-1].start()

    @pl.loop(0, rows // TILE)
    def _(j):
        col = pl.ds(pl.multiple_of(j * TILE, TILE), TILE)
        branch = lax.dot_general(
            act[...], w_out[col, :], (((1,), (1,)), ((), ())), preferred_element_type=F32
        )
        state_v[:, col] = (tok[:, col].astype(F32) + branch).astype(BF16)

    store_state = pltpu.make_async_copy(state_v, block_hbm, out_sems.at[1])
    store_state.start()

    stores = []
    for j in range(tiles):
        col = slice(j * TILE, (j + 1) * TILE)
        pairs[j].wait()
        pregrad[:, col] = ((slope_mine[j] + slope_other[j]) * pre_mine[j]).astype(BF16)
        gin_v[:, col] = lax.dot_general(
            normed[...], pregrad[:, col], (((0,), (0,)), ((), ())), preferred_element_type=F32
        ).astype(BF16)
        stores.append(
            pltpu.make_async_copy(gin_v.at[:, col], gin_hbm.at[:, col], out_sems.at[2 + j])
        )
        stores[-1].start()

    for step in steps:
        gather_copy(0, step, path_in, arr_in).wait_send()
        gather_copy(1, step, path_out, arr_out).wait_send()
        spread_copy(2, step, pick_in, w_in).wait_send()
        spread_copy(3, step, pick_out, w_out).wait_send()
    store_gout.wait()
    store_state.wait()
    for store in stores:
        store.wait()


def fused(
    tokens, cotangent, path_modules, path_in, path_out, outer_in, outer_out, moment_in, moment_out
):
    paths = lax.axis_size("path")
    mods = lax.axis_size("mod")
    rows, hidden = path_in.shape[2:]
    modules, owner = outer_in.shape[1:3]
    count = tokens.shape[1]
    tiles = hidden // TILE
    dims = (paths, modules, rows, owner, hidden, count, rows * mods)
    any_space = pl.BlockSpec(memory_space=pl.ANY)
    vmem = pltpu.VMEM
    out = pl.pallas_call(
        functools.partial(fused_kernel, dims),
        out_shape=(
            jax.ShapeDtypeStruct((count, rows), BF16),
            jax.ShapeDtypeStruct((rows, hidden), BF16),
            jax.ShapeDtypeStruct((rows, hidden), BF16),
        ),
        in_specs=[pl.BlockSpec(memory_space=pltpu.SMEM)] + [any_space] * 8,
        out_specs=(any_space,) * 3,
        scratch_shapes=[
            vmem((paths, owner, hidden), BF16),
            vmem((paths, owner, hidden), BF16),
            vmem((modules, owner, hidden), F32),
            vmem((modules, owner, hidden), F32),
            vmem((modules, owner, hidden), BF16),
            vmem((paths, owner, hidden), BF16),
            vmem((paths, owner, hidden), BF16),
            vmem((rows, hidden), BF16),
            vmem((rows, hidden), BF16),
            vmem((count, rows), BF16),
            vmem((count, rows), BF16),
            vmem((count, rows), BF16),
            vmem((count, 128), F32),
            vmem((count, 128), F32),
            vmem((tiles, count, TILE), F32),
            vmem((tiles, count, TILE), F32),
            vmem((tiles, count, TILE), F32),
            vmem((tiles, count, TILE), F32),
            vmem((count, hidden), BF16),
            vmem((count, hidden), BF16),
            vmem((rows, hidden), BF16),
            vmem((rows, hidden), BF16),
            vmem((count, rows), BF16),
            pltpu.SMEM((modules * paths,), F32),
            pltpu.SMEM((modules,), F32),
            pltpu.SemaphoreType.DMA((4, paths)),
            pltpu.SemaphoreType.DMA((4, paths)),
            pltpu.SemaphoreType.DMA((2,)),
            pltpu.SemaphoreType.DMA((2 + tiles,)),
            pltpu.SemaphoreType.DMA((2 + tiles,)),
            pltpu.SemaphoreType.DMA((4,)),
            pltpu.SemaphoreType.DMA((2 + tiles,)),
        ],
        compiler_params=pltpu.CompilerParams(
            collective_id=0, has_side_effects=True, vmem_limit_bytes=62 * 1024 * 1024
        ),
        cost_estimate=pl.CostEstimate(
            flops=10 * count * rows * hidden,
            bytes_accessed=8 * rows * hidden * 2,
            transcendentals=count * hidden,
        ),
    )(
        path_modules,
        tokens[0],
        cotangent[0],
        path_in[0, 0],
        path_out[0, 0],
        outer_in[0],
        outer_out[0],
        moment_in[0],
        moment_out[0],
    )
    state, grad_in, grad_out = out
    return (state[None], grad_in[None, None], grad_out[None, None])


def device_program(*arrays):
    level_count, rows, hidden = arrays[3].shape[1:]
    owner = arrays[5].shape[2]
    fits = (
        level_count == 1
        and lax.axis_size("mod") == 2
        and owner % 16 == 0
        and rows % TILE == 0
        and hidden % TILE == 0
        and arrays[0].shape[1] % 32 == 0
    )
    return fused(*arrays) if fits else local(*arrays)


def solution(mesh):
    return jax.shard_map(
        device_program,
        mesh=mesh,
        in_specs=(
            P("path", None, "mod"),
            P("path", None, "mod"),
            P(),
            P("path", None, "mod", None),
            P("path", None, "mod", None),
            P(None, None, ("mod", "path"), None),
            P(None, None, ("mod", "path"), None),
            P(None, None, ("mod", "path"), None),
            P(None, None, ("mod", "path"), None),
        ),
        out_specs=(
            P("path", None, "mod"),
            P("path", None, "mod", None),
            P("path", None, "mod", None),
        ),
        check_vma=False,
    )
```

```python
import functools

import jax
import jax.numpy as jnp
from jax import lax
from jax.experimental import pallas as pl
from jax.experimental.pallas import tpu as pltpu
from jax.sharding import PartitionSpec as P

D = 3072


epsilon = 1e-05
outer_rate = 0.7
outer_momentum = 0.9


def outer_step(outer, moment, average):
    delta = outer - average
    moment_next = outer_momentum * moment + delta
    return (outer - outer_rate * (delta + outer_momentum * moment_next)).astype(jnp.bfloat16)


def silu_slope(pre):
    sigmoid_z = jax.nn.sigmoid(pre)
    return sigmoid_z * (1.0 + pre * (1.0 - sigmoid_z))


def token_total(values):
    return lax.psum(values, "mod")


def share_total(left, right):
    return lax.psum_scatter(
        jnp.dot(left, right, preferred_element_type=jnp.float32),
        "mod",
        scatter_dimension=0,
        tiled=True,
    )


def share_gather(values):
    return lax.all_gather(values, "mod", axis=0, tiled=True)


def hidden_forward(normed, weight_level):
    pre_share = share_total(normed, weight_level)
    act_share = jax.nn.silu(pre_share).astype(jnp.bfloat16)
    return (pre_share, share_gather(act_share))


def hidden_backward(upstream, weight_level, pre):
    slope_share = share_total(upstream, weight_level)
    return share_gather((slope_share * silu_slope(pre)).astype(jnp.bfloat16))


def local(
    tokens, cotangent, path_modules, path_in, path_out, outer_in, outer_out, moment_in, moment_out
):
    path_count = lax.axis_size("path")
    level_count = path_in.shape[1]
    local_rows = path_in.shape[2]
    hidden = path_in.shape[3]
    module_count = outer_in.shape[1]
    owner_rows = outer_in.shape[2]
    piece_shape = (level_count, path_count, owner_rows, hidden)
    arrived_in, arrived_out = (
        lax.all_to_all(
            path_in.reshape(piece_shape), "path", split_axis=1, concat_axis=1, tiled=True
        ),
        lax.all_to_all(
            path_out.reshape(piece_shape), "path", split_axis=1, concat_axis=1, tiled=True
        ),
    )
    level = 0
    chosen = path_modules[:, level]
    member = chosen[None, :] == jnp.arange(module_count, dtype=jnp.int32)[:, None]
    counts = jnp.sum(member.astype(jnp.float32), axis=1)[:, None, None]
    member_bf = member.astype(jnp.bfloat16)
    summed_in = jnp.dot(
        member_bf,
        arrived_in[level].reshape(path_count, owner_rows * hidden),
        preferred_element_type=jnp.float32,
    )
    summed_out = jnp.dot(
        member_bf,
        arrived_out[level].reshape(path_count, owner_rows * hidden),
        preferred_element_type=jnp.float32,
    )
    fresh_in = outer_step(
        outer_in[level],
        moment_in[level],
        summed_in.reshape(module_count, owner_rows, hidden) / counts,
    )
    fresh_out = outer_step(
        outer_out[level],
        moment_out[level],
        summed_out.reshape(module_count, owner_rows, hidden) / counts,
    )
    picked_in = jnp.stack([jnp.take(fresh_in, path_modules[:, 0], axis=0)])
    picked_out = jnp.stack([jnp.take(fresh_out, path_modules[:, 0], axis=0)])
    back_in, back_out = (
        lax.all_to_all(picked_in, "path", split_axis=1, concat_axis=1, tiled=True),
        lax.all_to_all(picked_out, "path", split_axis=1, concat_axis=1, tiled=True),
    )
    weight_in = back_in.reshape(level_count, local_rows, hidden)
    weight_out = back_out.reshape(level_count, local_rows, hidden)
    state = tokens[0]
    level = 0
    wide = state.astype(jnp.float32)
    scale = lax.rsqrt(token_total(jnp.sum(wide * wide, axis=1)) / D + epsilon)[:, None]
    normal = wide * scale
    normed = normal.astype(jnp.bfloat16)
    pre, act = hidden_forward(normed, weight_in[level])
    branch = lax.dot_general(
        act, weight_out[level], (((1,), (1,)), ((), ())), preferred_element_type=jnp.float32
    )
    saved = [(scale, normal, normed, pre, act)]
    state = (wide + branch).astype(jnp.bfloat16)
    upstream = cotangent[0]
    grads_in = [None] * level_count
    grads_out = [None] * level_count
    for level in reversed(range(level_count)):
        scale, normal, normed, pre, act = saved[level]
        grads_out[level] = lax.dot_general(
            upstream, act, (((0,), (0,)), ((), ())), preferred_element_type=jnp.float32
        ).astype(jnp.bfloat16)
        pregrad = hidden_backward(upstream, weight_out[level], pre)
        grads_in[level] = lax.dot_general(
            normed, pregrad, (((0,), (0,)), ((), ())), preferred_element_type=jnp.float32
        ).astype(jnp.bfloat16)
    return (state[None], jnp.stack(grads_in)[None], jnp.stack(grads_out)[None])


MESH = pl.DeviceIdType.MESH
F32 = jnp.float32
BF16 = jnp.bfloat16
TILE = 256


def step_order(count):
    half = count // 2
    far, near = list(range(half, count)), list(range(1, half))
    order = []
    while far or near:
        order += far[:1] + near[:1]
        far, near = far[1:], near[1:]
    return order


def partner(me, step, count):
    if count & (count - 1):
        return lax.rem(me + step, count)
    other, bit = 0, 1
    while bit < count:
        other = other + bit * lax.rem(me // bit + (step // bit) % 2, 2)
        bit *= 2
    return other


def fused_kernel(
    dims,
    pm_ref,
    tok_hbm,
    cot_hbm,
    path_in,
    path_out,
    outer_in,
    outer_out,
    moment_in,
    moment_out,
    block_hbm,
    gin_hbm,
    gout_hbm,
    arr_in,
    arr_out,
    outer_v,
    moment_v,
    fresh,
    pick_in,
    pick_out,
    w_in,
    w_out,
    tok,
    cot,
    normed,
    norm_mine,
    norm_other,
    pre_mine,
    pre_other,
    slope_mine,
    slope_other,
    act,
    pregrad,
    gin_v,
    gout_v,
    state_v,
    member,
    count,
    send_sems,
    recv_sems,
    own_sems,
    pair_send,
    pair_recv,
    load_sems,
    out_sems,
):
    paths, modules, rows, owner, hidden, tokens, width = dims
    me = lax.axis_index("path")
    core = lax.axis_index("mod")
    steps = step_order(paths)
    tiles = hidden // TILE

    barrier = pltpu.get_barrier_semaphore()
    for step in steps:
        pl.semaphore_signal(
            barrier, inc=1, device_id=(partner(me, step, paths), core), device_id_type=MESH
        )
    pl.semaphore_signal(barrier, inc=1, device_id=(me, 1 - core), device_id_type=MESH)
    pl.semaphore_wait(barrier, paths)

    def span(index):
        return pl.ds(pl.multiple_of(index * owner, 16), owner)

    def gather_copy(kind, step, whole, arrived):
        dest = partner(me, step, paths)
        return pltpu.make_async_remote_copy(
            src_ref=whole.at[span(dest)],
            dst_ref=arrived.at[me],
            send_sem=send_sems.at[kind, step],
            recv_sem=recv_sems.at[kind, step],
            device_id=(dest, core),
            device_id_type=MESH,
        )

    def spread_copy(kind, step, picked, weight):
        dest = partner(me, step, paths)
        return pltpu.make_async_remote_copy(
            src_ref=picked.at[dest],
            dst_ref=weight.at[span(me)],
            send_sem=send_sems.at[kind, step],
            recv_sem=recv_sems.at[kind, step],
            device_id=(dest, core),
            device_id_type=MESH,
        )

    def pair_copy(slot, source, target):
        return pltpu.make_async_remote_copy(
            src_ref=source,
            dst_ref=target,
            send_sem=pair_send.at[slot],
            recv_sem=pair_recv.at[slot],
            device_id=(me, 1 - core),
            device_id_type=MESH,
        )

    for step in steps:
        gather_copy(0, step, path_in, arr_in).start()
    for step in steps:
        gather_copy(1, step, path_out, arr_out).start()

    own_in = pltpu.make_async_copy(path_in.at[span(me)], arr_in.at[me], own_sems.at[0])
    own_out = pltpu.make_async_copy(path_out.at[span(me)], arr_out.at[me], own_sems.at[1])
    load_tok = pltpu.make_async_copy(tok_hbm, tok, load_sems.at[0])
    load_cot = pltpu.make_async_copy(cot_hbm, cot, load_sems.at[1])
    load_outer = pltpu.make_async_copy(outer_in, outer_v, load_sems.at[2])
    load_moment = pltpu.make_async_copy(moment_in, moment_v, load_sems.at[3])
    for copy in (load_tok, load_cot, own_in, own_out, load_outer, load_moment):
        copy.start()

    for k in range(modules):
        total = jnp.float32(0.0)
        for p in range(paths):
            flag = jnp.where(pm_ref[p, 0] == k, jnp.float32(1.0), jnp.float32(0.0))
            member[k * paths + p] = flag
            total = total + flag
        count[k] = total

    load_tok.wait()
    block = 32

    @pl.loop(0, tokens // block)
    def _(i):
        at = pl.ds(pl.multiple_of(i * block, block), block)
        wide = tok[at, :].astype(F32)
        norm_mine[at, :] = jnp.broadcast_to(
            jnp.sum(wide * wide, axis=1, keepdims=True), (block, 128)
        )

    pair = pair_copy(0, norm_mine, norm_other)
    pair.start()
    pair.wait()

    @pl.loop(0, tokens // block)
    def _(i):
        at = pl.ds(pl.multiple_of(i * block, block), block)
        total = norm_mine[at, :][:, :1] + norm_other[at, :][:, :1]
        scale = lax.rsqrt(total / width + epsilon)
        normed[at, :] = (tok[at, :].astype(F32) * scale).astype(BF16)

    load_cot.wait()

    def update(arrived):
        columns = hidden // TILE

        @pl.loop(0, (owner // 16) * columns)
        def _(i):
            at = pl.ds(pl.multiple_of((i // columns) * 16, 16), 16)
            col = pl.ds(pl.multiple_of((i % columns) * TILE, TILE), TILE)
            sums = [jnp.zeros((16, TILE), F32) for _ in range(modules)]
            for p in range(paths):
                x = arrived[p, at, col].astype(F32)
                for k in range(modules):
                    sums[k] = sums[k] + member[k * paths + p] * x
            for k in range(modules):
                average = sums[k] / count[k]
                fresh[k, at, col] = outer_step(
                    outer_v[k, at, col], moment_v[k, at, col], average
                )

    def spread(kind, picked, weight):
        for step in steps:
            dest = partner(me, step, paths)
            picked[dest] = fresh[pm_ref[dest, 0]]
            spread_copy(kind, step, picked, weight).start()
        weight[span(me), :] = fresh[pm_ref[me, 0]]

    own_in.wait()
    load_outer.wait()
    load_moment.wait()
    for step in steps:
        gather_copy(0, step, path_in, arr_in).wait_recv()
    update(arr_in)
    load_outer = pltpu.make_async_copy(outer_out, outer_v, load_sems.at[2])
    load_moment = pltpu.make_async_copy(moment_out, moment_v, load_sems.at[3])
    load_outer.start()
    load_moment.start()
    spread(2, pick_in, w_in)

    own_out.wait()
    load_outer.wait()
    load_moment.wait()
    for step in steps:
        gather_copy(1, step, path_out, arr_out).wait_recv()
    update(arr_out)
    spread(3, pick_out, w_out)

    for step in steps:
        spread_copy(2, step, pick_in, w_in).wait_recv()

    @pl.loop(0, tiles)
    def _(j):
        col = pl.ds(pl.multiple_of(j * TILE, TILE), TILE)
        pre_mine[j] = jnp.dot(normed[...], w_in[:, col], preferred_element_type=F32)

    pair = pair_copy(1, pre_mine, pre_other)
    pair.start()
    pair.wait()

    for j in range(tiles):

        @pl.loop(0, tokens // block)
        def _(i):
            at = pl.ds(pl.multiple_of(i * block, block), block)
            pre = pre_mine[j, at, :] + pre_other[j, at, :]
            sigmoid = jax.nn.sigmoid(pre)
            act[at, j * TILE : (j + 1) * TILE] = (pre * sigmoid).astype(BF16)
            pre_mine[j, at, :] = sigmoid * (1.0 + pre * (1.0 - sigmoid))

    @pl.loop(0, tiles)
    def _(j):
        col = pl.ds(pl.multiple_of(j * TILE, TILE), TILE)
        gout_v[:, col] = lax.dot_general(
            cot[...], act[:, col], (((0,), (0,)), ((), ())), preferred_element_type=F32
        ).astype(BF16)

    store_gout = pltpu.make_async_copy(gout_v, gout_hbm, out_sems.at[0])
    store_gout.start()

    for step in steps:
        spread_copy(3, step, pick_out, w_out).wait_recv()

    pairs = []
    for j in range(tiles):
        slope_mine[j] = jnp.dot(
            cot[...], w_out[:, j * TILE : (j + 1) * TILE], preferred_element_type=F32
        )
        pairs.append(pair_copy(2 + j, slope_mine.at[j], slope_other.at[j]))
        pairs[-1].start()

    @pl.loop(0, rows // TILE)
    def _(j):
        col = pl.ds(pl.multiple_of(j * TILE, TILE), TILE)
        branch = lax.dot_general(
            act[...], w_out[col, :], (((1,), (1,)), ((), ())), preferred_element_type=F32
        )
        state_v[:, col] = (tok[:, col].astype(F32) + branch).astype(BF16)

    store_state = pltpu.make_async_copy(state_v, block_hbm, out_sems.at[1])
    store_state.start()

    stores = []
    for j in range(tiles):
        col = slice(j * TILE, (j + 1) * TILE)
        pairs[j].wait()
        pregrad[:, col] = ((slope_mine[j] + slope_other[j]) * pre_mine[j]).astype(BF16)
        gin_v[:, col] = lax.dot_general(
            normed[...], pregrad[:, col], (((0,), (0,)), ((), ())), preferred_element_type=F32
        ).astype(BF16)
        stores.append(
            pltpu.make_async_copy(gin_v.at[:, col], gin_hbm.at[:, col], out_sems.at[2 + j])
        )
        stores[-1].start()

    for step in steps:
        gather_copy(0, step, path_in, arr_in).wait_send()
        gather_copy(1, step, path_out, arr_out).wait_send()
        spread_copy(2, step, pick_in, w_in).wait_send()
        spread_copy(3, step, pick_out, w_out).wait_send()
    store_gout.wait()
    store_state.wait()
    for store in stores:
        store.wait()


def fused(
    tokens, cotangent, path_modules, path_in, path_out, outer_in, outer_out, moment_in, moment_out
):
    paths = lax.axis_size("path")
    mods = lax.axis_size("mod")
    rows, hidden = path_in.shape[2:]
    modules, owner = outer_in.shape[1:3]
    count = tokens.shape[1]
    tiles = hidden // TILE
    dims = (paths, modules, rows, owner, hidden, count, rows * mods)
    any_space = pl.BlockSpec(memory_space=pl.ANY)
    vmem = pltpu.VMEM
    out = pl.pallas_call(
        functools.partial(fused_kernel, dims),
        out_shape=(
            jax.ShapeDtypeStruct((count, rows), BF16),
            jax.ShapeDtypeStruct((rows, hidden), BF16),
            jax.ShapeDtypeStruct((rows, hidden), BF16),
        ),
        in_specs=[pl.BlockSpec(memory_space=pltpu.SMEM)] + [any_space] * 8,
        out_specs=(any_space,) * 3,
        scratch_shapes=[
            vmem((paths, owner, hidden), BF16),
            vmem((paths, owner, hidden), BF16),
            vmem((modules, owner, hidden), F32),
            vmem((modules, owner, hidden), F32),
            vmem((modules, owner, hidden), BF16),
            vmem((paths, owner, hidden), BF16),
            vmem((paths, owner, hidden), BF16),
            vmem((rows, hidden), BF16),
            vmem((rows, hidden), BF16),
            vmem((count, rows), BF16),
            vmem((count, rows), BF16),
            vmem((count, rows), BF16),
            vmem((count, 128), F32),
            vmem((count, 128), F32),
            vmem((tiles, count, TILE), F32),
            vmem((tiles, count, TILE), F32),
            vmem((tiles, count, TILE), F32),
            vmem((tiles, count, TILE), F32),
            vmem((count, hidden), BF16),
            vmem((count, hidden), BF16),
            vmem((rows, hidden), BF16),
            vmem((rows, hidden), BF16),
            vmem((count, rows), BF16),
            pltpu.SMEM((modules * paths,), F32),
            pltpu.SMEM((modules,), F32),
            pltpu.SemaphoreType.DMA((4, paths)),
            pltpu.SemaphoreType.DMA((4, paths)),
            pltpu.SemaphoreType.DMA((2,)),
            pltpu.SemaphoreType.DMA((2 + tiles,)),
            pltpu.SemaphoreType.DMA((2 + tiles,)),
            pltpu.SemaphoreType.DMA((4,)),
            pltpu.SemaphoreType.DMA((2 + tiles,)),
        ],
        compiler_params=pltpu.CompilerParams(
            collective_id=0, has_side_effects=True, vmem_limit_bytes=62 * 1024 * 1024
        ),
        cost_estimate=pl.CostEstimate(
            flops=10 * count * rows * hidden,
            bytes_accessed=8 * rows * hidden * 2,
            transcendentals=count * hidden,
        ),
    )(
        path_modules,
        tokens[0],
        cotangent[0],
        path_in[0, 0],
        path_out[0, 0],
        outer_in[0],
        outer_out[0],
        moment_in[0],
        moment_out[0],
    )
    state, grad_in, grad_out = out
    return (state[None], grad_in[None, None], grad_out[None, None])


def device_program(*arrays):
    level_count, rows, hidden = arrays[3].shape[1:]
    owner = arrays[5].shape[2]
    fits = (
        level_count == 1
        and lax.axis_size("mod") == 2
        and owner % 16 == 0
        and rows % TILE == 0
        and hidden % TILE == 0
        and arrays[0].shape[1] % 32 == 0
    )
    return fused(*arrays) if fits else local(*arrays)


def solution(mesh):
    return jax.shard_map(
        device_program,
        mesh=mesh,
        in_specs=(
            P("path", None, "mod"),
            P("path", None, "mod"),
            P(),
            P("path", None, "mod", None),
            P("path", None, "mod", None),
            P(None, None, ("mod", "path"), None),
            P(None, None, ("mod", "path"), None),
            P(None, None, ("mod", "path"), None),
            P(None, None, ("mod", "path"), None),
        ),
        out_specs=(
            P("path", None, "mod"),
            P("path", None, "mod", None),
            P("path", None, "mod", None),
        ),
        check_vma=False,
    )
```

```python
import functools

import jax
import jax.numpy as jnp
from jax import lax
from jax.experimental import pallas as pl
from jax.experimental.pallas import tpu as pltpu
from jax.sharding import PartitionSpec as P

D = 3072


epsilon = 1e-05
outer_rate = 0.7
outer_momentum = 0.9


def outer_step(outer, moment, average):
    delta = outer - average
    moment_next = outer_momentum * moment + delta
    return (outer - outer_rate * (delta + outer_momentum * moment_next)).astype(jnp.bfloat16)


def silu_slope(pre):
    sigmoid_z = jax.nn.sigmoid(pre)
    return sigmoid_z * (1.0 + pre * (1.0 - sigmoid_z))


def token_total(values):
    return lax.psum(values, "mod")


def share_total(left, right):
    return lax.psum_scatter(
        jnp.dot(left, right, preferred_element_type=jnp.float32),
        "mod",
        scatter_dimension=0,
        tiled=True,
    )


def share_gather(values):
    return lax.all_gather(values, "mod", axis=0, tiled=True)


def hidden_forward(normed, weight_level):
    pre_share = share_total(normed, weight_level)
    act_share = jax.nn.silu(pre_share).astype(jnp.bfloat16)
    return (pre_share, share_gather(act_share))


def hidden_backward(upstream, weight_level, pre):
    slope_share = share_total(upstream, weight_level)
    return share_gather((slope_share * silu_slope(pre)).astype(jnp.bfloat16))


def local(
    tokens, cotangent, path_modules, path_in, path_out, outer_in, outer_out, moment_in, moment_out
):
    path_count = lax.axis_size("path")
    level_count = path_in.shape[1]
    local_rows = path_in.shape[2]
    hidden = path_in.shape[3]
    module_count = outer_in.shape[1]
    owner_rows = outer_in.shape[2]
    piece_shape = (level_count, path_count, owner_rows, hidden)
    arrived_in, arrived_out = (
        lax.all_to_all(
            path_in.reshape(piece_shape), "path", split_axis=1, concat_axis=1, tiled=True
        ),
        lax.all_to_all(
            path_out.reshape(piece_shape), "path", split_axis=1, concat_axis=1, tiled=True
        ),
    )
    level = 0
    chosen = path_modules[:, level]
    member = chosen[None, :] == jnp.arange(module_count, dtype=jnp.int32)[:, None]
    counts = jnp.sum(member.astype(jnp.float32), axis=1)[:, None, None]
    member_bf = member.astype(jnp.bfloat16)
    summed_in = jnp.dot(
        member_bf,
        arrived_in[level].reshape(path_count, owner_rows * hidden),
        preferred_element_type=jnp.float32,
    )
    summed_out = jnp.dot(
        member_bf,
        arrived_out[level].reshape(path_count, owner_rows * hidden),
        preferred_element_type=jnp.float32,
    )
    fresh_in = outer_step(
        outer_in[level],
        moment_in[level],
        summed_in.reshape(module_count, owner_rows, hidden) / counts,
    )
    fresh_out = outer_step(
        outer_out[level],
        moment_out[level],
        summed_out.reshape(module_count, owner_rows, hidden) / counts,
    )
    picked_in = jnp.stack([jnp.take(fresh_in, path_modules[:, 0], axis=0)])
    picked_out = jnp.stack([jnp.take(fresh_out, path_modules[:, 0], axis=0)])
    back_in, back_out = (
        lax.all_to_all(picked_in, "path", split_axis=1, concat_axis=1, tiled=True),
        lax.all_to_all(picked_out, "path", split_axis=1, concat_axis=1, tiled=True),
    )
    weight_in = back_in.reshape(level_count, local_rows, hidden)
    weight_out = back_out.reshape(level_count, local_rows, hidden)
    state = tokens[0]
    level = 0
    wide = state.astype(jnp.float32)
    scale = lax.rsqrt(token_total(jnp.sum(wide * wide, axis=1)) / D + epsilon)[:, None]
    normal = wide * scale
    normed = normal.astype(jnp.bfloat16)
    pre, act = hidden_forward(normed, weight_in[level])
    branch = lax.dot_general(
        act, weight_out[level], (((1,), (1,)), ((), ())), preferred_element_type=jnp.float32
    )
    saved = [(scale, normal, normed, pre, act)]
    state = (wide + branch).astype(jnp.bfloat16)
    upstream = cotangent[0]
    grads_in = [None] * level_count
    grads_out = [None] * level_count
    for level in reversed(range(level_count)):
        scale, normal, normed, pre, act = saved[level]
        grads_out[level] = lax.dot_general(
            upstream, act, (((0,), (0,)), ((), ())), preferred_element_type=jnp.float32
        ).astype(jnp.bfloat16)
        pregrad = hidden_backward(upstream, weight_out[level], pre)
        grads_in[level] = lax.dot_general(
            normed, pregrad, (((0,), (0,)), ((), ())), preferred_element_type=jnp.float32
        ).astype(jnp.bfloat16)
    return (state[None], jnp.stack(grads_in)[None], jnp.stack(grads_out)[None])


MESH = pl.DeviceIdType.MESH
F32 = jnp.float32
BF16 = jnp.bfloat16
TILE = 256


def step_order(count):
    half = count // 2
    far, near = list(range(half, count)), list(range(1, half))
    order = []
    while far or near:
        order += far[:1] + near[:1]
        far, near = far[1:], near[1:]
    return order


def partner(me, step, count):
    if count & (count - 1):
        return lax.rem(me + step, count)
    other, bit = 0, 1
    while bit < count:
        other = other + bit * lax.rem(me // bit + (step // bit) % 2, 2)
        bit *= 2
    return other


def fused_kernel(
    dims,
    pm_ref,
    tok_hbm,
    cot_hbm,
    path_in,
    path_out,
    outer_in,
    outer_out,
    moment_in,
    moment_out,
    block_hbm,
    act_hbm,
    pregrad_hbm,
    normed_t_hbm,
    cot_t_hbm,
    arr_in,
    arr_out,
    outer_v,
    moment_v,
    fresh,
    pick_in,
    pick_out,
    w_in,
    w_out,
    tok,
    cot,
    normed,
    norm_mine,
    norm_other,
    pre_mine,
    pre_other,
    slope_mine,
    slope_sent,
    slope_other,
    act,
    pregrad,
    normed_t,
    cot_t,
    state_v,
    member,
    count,
    send_sems,
    recv_sems,
    own_sems,
    pair_send,
    pair_recv,
    load_sems,
    out_sems,
):
    paths, modules, rows, owner, hidden, tokens, width = dims
    me = lax.axis_index("path")
    core = lax.axis_index("mod")
    steps = step_order(paths)
    tiles = hidden // TILE

    barrier = pltpu.get_barrier_semaphore()
    for step in steps:
        pl.semaphore_signal(
            barrier, inc=1, device_id=(partner(me, step, paths), core), device_id_type=MESH
        )
    pl.semaphore_signal(barrier, inc=1, device_id=(me, 1 - core), device_id_type=MESH)
    pl.semaphore_wait(barrier, paths)

    def span(index):
        return pl.ds(pl.multiple_of(index * owner, 16), owner)

    def gather_copy(kind, step, whole, arrived):
        dest = partner(me, step, paths)
        return pltpu.make_async_remote_copy(
            src_ref=whole.at[span(dest)],
            dst_ref=arrived.at[me],
            send_sem=send_sems.at[kind, step],
            recv_sem=recv_sems.at[kind, step],
            device_id=(dest, core),
            device_id_type=MESH,
        )

    def spread_copy(kind, step, picked, weight):
        dest = partner(me, step, paths)
        return pltpu.make_async_remote_copy(
            src_ref=picked.at[dest],
            dst_ref=weight.at[span(me)],
            send_sem=send_sems.at[kind, step],
            recv_sem=recv_sems.at[kind, step],
            device_id=(dest, core),
            device_id_type=MESH,
        )

    def pair_copy(slot, source, target):
        return pltpu.make_async_remote_copy(
            src_ref=source,
            dst_ref=target,
            send_sem=pair_send.at[slot],
            recv_sem=pair_recv.at[slot],
            device_id=(me, 1 - core),
            device_id_type=MESH,
        )

    for step in steps:
        gather_copy(0, step, path_in, arr_in).start()
    for step in steps:
        gather_copy(1, step, path_out, arr_out).start()

    own_in = pltpu.make_async_copy(path_in.at[span(me)], arr_in.at[me], own_sems.at[0])
    own_out = pltpu.make_async_copy(path_out.at[span(me)], arr_out.at[me], own_sems.at[1])
    load_tok = pltpu.make_async_copy(tok_hbm, tok, load_sems.at[0])
    load_cot = pltpu.make_async_copy(cot_hbm, cot, load_sems.at[1])
    load_outer = pltpu.make_async_copy(outer_in, outer_v, load_sems.at[2])
    load_moment = pltpu.make_async_copy(moment_in, moment_v, load_sems.at[3])
    for copy in (load_tok, load_cot, own_in, own_out, load_outer, load_moment):
        copy.start()

    for k in range(modules):
        total = jnp.float32(0.0)
        for p in range(paths):
            flag = jnp.where(pm_ref[p, 0] == k, jnp.float32(1.0), jnp.float32(0.0))
            member[k * paths + p] = flag
            total = total + flag
        count[k] = total

    load_tok.wait()
    block = 32

    @pl.loop(0, tokens // block)
    def _(i):
        at = pl.ds(pl.multiple_of(i * block, block), block)
        wide = tok[at, :].astype(F32)
        norm_mine[at, :] = jnp.broadcast_to(
            jnp.sum(wide * wide, axis=1, keepdims=True), (block, 128)
        )

    pair = pair_copy(0, norm_mine, norm_other)
    pair.start()
    pair.wait()

    @pl.loop(0, tokens // block)
    def _(i):
        at = pl.ds(pl.multiple_of(i * block, block), block)
        total = norm_mine[at, :][:, :1] + norm_other[at, :][:, :1]
        scale = lax.rsqrt(total / width + epsilon)
        normed[at, :] = (tok[at, :].astype(F32) * scale).astype(BF16)

    load_cot.wait()

    @pl.loop(0, rows // TILE)
    def _(j):
        col = pl.ds(pl.multiple_of(j * TILE, TILE), TILE)
        normed_t[col, :] = normed[:, col].astype(F32).T.astype(BF16)
        cot_t[col, :] = cot[:, col].astype(F32).T.astype(BF16)

    stores = [
        pltpu.make_async_copy(normed_t, normed_t_hbm, out_sems.at[0]),
        pltpu.make_async_copy(cot_t, cot_t_hbm, out_sems.at[1]),
    ]
    for store in stores:
        store.start()

    def update(arrived):
        columns = hidden // TILE

        @pl.loop(0, (owner // 16) * columns)
        def _(i):
            at = pl.ds(pl.multiple_of((i // columns) * 16, 16), 16)
            col = pl.ds(pl.multiple_of((i % columns) * TILE, TILE), TILE)
            sums = [jnp.zeros((16, TILE), F32) for _ in range(modules)]
            for p in range(paths):
                x = arrived[p, at, col].astype(F32)
                for k in range(modules):
                    sums[k] = sums[k] + member[k * paths + p] * x
            for k in range(modules):
                average = sums[k] / count[k]
                fresh[k, at, col] = outer_step(
                    outer_v[k, at, col], moment_v[k, at, col], average
                )

    def spread(kind, picked, weight):
        for step in steps:
            dest = partner(me, step, paths)
            picked[dest] = fresh[pm_ref[dest, 0]]
            spread_copy(kind, step, picked, weight).start()
        weight[span(me), :] = fresh[pm_ref[me, 0]]

    own_in.wait()
    load_outer.wait()
    load_moment.wait()
    for step in steps:
        gather_copy(0, step, path_in, arr_in).wait_recv()
    update(arr_in)
    load_outer = pltpu.make_async_copy(outer_out, outer_v, load_sems.at[2])
    load_moment = pltpu.make_async_copy(moment_out, moment_v, load_sems.at[3])
    load_outer.start()
    load_moment.start()
    spread(2, pick_in, w_in)

    own_out.wait()
    load_outer.wait()
    load_moment.wait()
    for step in steps:
        gather_copy(1, step, path_out, arr_out).wait_recv()
    update(arr_out)
    spread(3, pick_out, w_out)

    for step in steps:
        spread_copy(2, step, pick_in, w_in).wait_recv()

    @pl.loop(0, tiles)
    def _(j):
        col = pl.ds(pl.multiple_of(j * TILE, TILE), TILE)
        pre_mine[j] = jnp.dot(normed[...], w_in[:, col], preferred_element_type=F32)

    pair = pair_copy(1, pre_mine, pre_other)
    pair.start()
    pair.wait()

    for j in range(tiles):

        @pl.loop(0, tokens // block)
        def _(i):
            at = pl.ds(pl.multiple_of(i * block, block), block)
            pre = pre_mine[j, at, :] + pre_other[j, at, :]
            sigmoid = jax.nn.sigmoid(pre)
            act[at, j * TILE : (j + 1) * TILE] = (pre * sigmoid).astype(BF16)
            pre_mine[j, at, :] = sigmoid * (1.0 + pre * (1.0 - sigmoid))

    stores.append(pltpu.make_async_copy(act, act_hbm, out_sems.at[2]))
    stores[-1].start()

    for step in steps:
        spread_copy(3, step, pick_out, w_out).wait_recv()

    pairs = []
    for j in range(tiles):
        slope_mine[j] = jnp.dot(
            cot[...], w_out[:, j * TILE : (j + 1) * TILE], preferred_element_type=F32
        )
        slope_sent[j] = slope_mine[j].astype(BF16)
        pairs.append(pair_copy(2 + j, slope_sent.at[j], slope_other.at[j]))
        pairs[-1].start()

    @pl.loop(0, rows // TILE)
    def _(j):
        col = pl.ds(pl.multiple_of(j * TILE, TILE), TILE)
        branch = lax.dot_general(
            act[...], w_out[col, :], (((1,), (1,)), ((), ())), preferred_element_type=F32
        )
        state_v[:, col] = (tok[:, col].astype(F32) + branch).astype(BF16)

    stores.append(pltpu.make_async_copy(state_v, block_hbm, out_sems.at[3]))
    stores[-1].start()

    for j in range(tiles):
        col = slice(j * TILE, (j + 1) * TILE)
        pairs[j].wait()
        slope = slope_mine[j] + slope_other[j].astype(F32)
        pregrad[:, col] = (slope * pre_mine[j]).astype(BF16)

    stores.append(pltpu.make_async_copy(pregrad, pregrad_hbm, out_sems.at[4]))
    stores[-1].start()

    for step in steps:
        gather_copy(0, step, path_in, arr_in).wait_send()
        gather_copy(1, step, path_out, arr_out).wait_send()
        spread_copy(2, step, pick_in, w_in).wait_send()
        spread_copy(3, step, pick_out, w_out).wait_send()
    for store in stores:
        store.wait()


def finish_kernel(state, act, pregrad, normed_t, cot_t, block_out, grad_in, grad_out):
    block_out[...] = state[...]
    grad_in[...] = jnp.dot(normed_t[...], pregrad[...], preferred_element_type=F32).astype(BF16)
    grad_out[...] = jnp.dot(cot_t[...], act[...], preferred_element_type=F32).astype(BF16)


def finish(state, act, pregrad, normed_t, cot_t):
    count, rows = state.shape
    hidden = act.shape[1]
    steps = rows // TILE

    def split(height, length):
        return pl.BlockSpec((height, length), lambda i: (i, 0))

    def whole(height, length):
        return pl.BlockSpec((height, length), lambda i: (0, 0))

    state_spec = pl.BlockSpec((count, TILE), lambda i: (0, i))
    return pl.pallas_call(
        finish_kernel,
        grid=(steps,),
        out_shape=(
            jax.ShapeDtypeStruct((count, rows), BF16),
            jax.ShapeDtypeStruct((rows, hidden), BF16),
            jax.ShapeDtypeStruct((rows, hidden), BF16),
        ),
        in_specs=[
            state_spec,
            whole(count, hidden),
            whole(count, hidden),
            split(TILE, count),
            split(TILE, count),
        ],
        out_specs=(state_spec, split(TILE, hidden), split(TILE, hidden)),
        compiler_params=pltpu.CompilerParams(vmem_limit_bytes=62 * 1024 * 1024),
        cost_estimate=pl.CostEstimate(
            flops=4 * count * rows * hidden,
            bytes_accessed=4 * rows * hidden + 8 * count * rows + 4 * count * hidden,
            transcendentals=0,
        ),
    )(state, act, pregrad, normed_t, cot_t)


def fused(
    tokens, cotangent, path_modules, path_in, path_out, outer_in, outer_out, moment_in, moment_out
):
    paths = lax.axis_size("path")
    mods = lax.axis_size("mod")
    rows, hidden = path_in.shape[2:]
    modules, owner = outer_in.shape[1:3]
    count = tokens.shape[1]
    tiles = hidden // TILE
    dims = (paths, modules, rows, owner, hidden, count, rows * mods)
    any_space = pl.BlockSpec(memory_space=pl.ANY)
    vmem = pltpu.VMEM
    out = pl.pallas_call(
        functools.partial(fused_kernel, dims),
        out_shape=(
            jax.ShapeDtypeStruct((count, rows), BF16),
            jax.ShapeDtypeStruct((count, hidden), BF16),
            jax.ShapeDtypeStruct((count, hidden), BF16),
            jax.ShapeDtypeStruct((rows, count), BF16),
            jax.ShapeDtypeStruct((rows, count), BF16),
        ),
        in_specs=[pl.BlockSpec(memory_space=pltpu.SMEM)] + [any_space] * 8,
        out_specs=(any_space,) * 5,
        scratch_shapes=[
            vmem((paths, owner, hidden), BF16),
            vmem((paths, owner, hidden), BF16),
            vmem((modules, owner, hidden), F32),
            vmem((modules, owner, hidden), F32),
            vmem((modules, owner, hidden), BF16),
            vmem((paths, owner, hidden), BF16),
            vmem((paths, owner, hidden), BF16),
            vmem((rows, hidden), BF16),
            vmem((rows, hidden), BF16),
            vmem((count, rows), BF16),
            vmem((count, rows), BF16),
            vmem((count, rows), BF16),
            vmem((count, 128), F32),
            vmem((count, 128), F32),
            vmem((tiles, count, TILE), F32),
            vmem((tiles, count, TILE), F32),
            vmem((tiles, count, TILE), F32),
            vmem((tiles, count, TILE), BF16),
            vmem((tiles, count, TILE), BF16),
            vmem((count, hidden), BF16),
            vmem((count, hidden), BF16),
            vmem((rows, count), BF16),
            vmem((rows, count), BF16),
            vmem((count, rows), BF16),
            pltpu.SMEM((modules * paths,), F32),
            pltpu.SMEM((modules,), F32),
            pltpu.SemaphoreType.DMA((4, paths)),
            pltpu.SemaphoreType.DMA((4, paths)),
            pltpu.SemaphoreType.DMA((2,)),
            pltpu.SemaphoreType.DMA((2 + tiles,)),
            pltpu.SemaphoreType.DMA((2 + tiles,)),
            pltpu.SemaphoreType.DMA((4,)),
            pltpu.SemaphoreType.DMA((5,)),
        ],
        compiler_params=pltpu.CompilerParams(
            collective_id=0, has_side_effects=True, vmem_limit_bytes=62 * 1024 * 1024
        ),
        cost_estimate=pl.CostEstimate(
            flops=10 * count * rows * hidden,
            bytes_accessed=8 * rows * hidden * 2,
            transcendentals=count * hidden,
        ),
    )(
        path_modules,
        tokens[0],
        cotangent[0],
        path_in[0, 0],
        path_out[0, 0],
        outer_in[0],
        outer_out[0],
        moment_in[0],
        moment_out[0],
    )
    state, grad_in, grad_out = finish(*out)
    return (state[None], grad_in[None, None], grad_out[None, None])


def device_program(*arrays):
    level_count, rows, hidden = arrays[3].shape[1:]
    owner = arrays[5].shape[2]
    fits = (
        level_count == 1
        and lax.axis_size("mod") == 2
        and owner % 16 == 0
        and rows % TILE == 0
        and hidden % TILE == 0
        and arrays[0].shape[1] % 32 == 0
    )
    return fused(*arrays) if fits else local(*arrays)


def solution(mesh):
    return jax.shard_map(
        device_program,
        mesh=mesh,
        in_specs=(
            P("path", None, "mod"),
            P("path", None, "mod"),
            P(),
            P("path", None, "mod", None),
            P("path", None, "mod", None),
            P(None, None, ("mod", "path"), None),
            P(None, None, ("mod", "path"), None),
            P(None, None, ("mod", "path"), None),
            P(None, None, ("mod", "path"), None),
        ),
        out_specs=(
            P("path", None, "mod"),
            P("path", None, "mod", None),
            P("path", None, "mod", None),
        ),
        check_vma=False,
    )
```

```python
import functools

import jax
import jax.numpy as jnp
from jax import lax
from jax.experimental import pallas as pl
from jax.experimental.pallas import tpu as pltpu
from jax.sharding import PartitionSpec as P

D = 3072


epsilon = 1e-05
outer_rate = 0.7
outer_momentum = 0.9


def outer_step(outer, moment, average):
    delta = outer - average
    moment_next = outer_momentum * moment + delta
    return (outer - outer_rate * (delta + outer_momentum * moment_next)).astype(jnp.bfloat16)


def silu_slope(pre):
    sigmoid_z = jax.nn.sigmoid(pre)
    return sigmoid_z * (1.0 + pre * (1.0 - sigmoid_z))


def token_total(values):
    return lax.psum(values, "mod")


def share_total(left, right):
    return lax.psum_scatter(
        jnp.dot(left, right, preferred_element_type=jnp.float32),
        "mod",
        scatter_dimension=0,
        tiled=True,
    )


def share_gather(values):
    return lax.all_gather(values, "mod", axis=0, tiled=True)


def hidden_forward(normed, weight_level):
    pre_share = share_total(normed, weight_level)
    act_share = jax.nn.silu(pre_share).astype(jnp.bfloat16)
    return (pre_share, share_gather(act_share))


def hidden_backward(upstream, weight_level, pre):
    slope_share = share_total(upstream, weight_level)
    return share_gather((slope_share * silu_slope(pre)).astype(jnp.bfloat16))


def local(
    tokens, cotangent, path_modules, path_in, path_out, outer_in, outer_out, moment_in, moment_out
):
    path_count = lax.axis_size("path")
    level_count = path_in.shape[1]
    local_rows = path_in.shape[2]
    hidden = path_in.shape[3]
    module_count = outer_in.shape[1]
    owner_rows = outer_in.shape[2]
    piece_shape = (level_count, path_count, owner_rows, hidden)
    arrived_in, arrived_out = (
        lax.all_to_all(
            path_in.reshape(piece_shape), "path", split_axis=1, concat_axis=1, tiled=True
        ),
        lax.all_to_all(
            path_out.reshape(piece_shape), "path", split_axis=1, concat_axis=1, tiled=True
        ),
    )
    level = 0
    chosen = path_modules[:, level]
    member = chosen[None, :] == jnp.arange(module_count, dtype=jnp.int32)[:, None]
    counts = jnp.sum(member.astype(jnp.float32), axis=1)[:, None, None]
    member_bf = member.astype(jnp.bfloat16)
    summed_in = jnp.dot(
        member_bf,
        arrived_in[level].reshape(path_count, owner_rows * hidden),
        preferred_element_type=jnp.float32,
    )
    summed_out = jnp.dot(
        member_bf,
        arrived_out[level].reshape(path_count, owner_rows * hidden),
        preferred_element_type=jnp.float32,
    )
    fresh_in = outer_step(
        outer_in[level],
        moment_in[level],
        summed_in.reshape(module_count, owner_rows, hidden) / counts,
    )
    fresh_out = outer_step(
        outer_out[level],
        moment_out[level],
        summed_out.reshape(module_count, owner_rows, hidden) / counts,
    )
    picked_in = jnp.stack([jnp.take(fresh_in, path_modules[:, 0], axis=0)])
    picked_out = jnp.stack([jnp.take(fresh_out, path_modules[:, 0], axis=0)])
    back_in, back_out = (
        lax.all_to_all(picked_in, "path", split_axis=1, concat_axis=1, tiled=True),
        lax.all_to_all(picked_out, "path", split_axis=1, concat_axis=1, tiled=True),
    )
    weight_in = back_in.reshape(level_count, local_rows, hidden)
    weight_out = back_out.reshape(level_count, local_rows, hidden)
    state = tokens[0]
    level = 0
    wide = state.astype(jnp.float32)
    scale = lax.rsqrt(token_total(jnp.sum(wide * wide, axis=1)) / D + epsilon)[:, None]
    normal = wide * scale
    normed = normal.astype(jnp.bfloat16)
    pre, act = hidden_forward(normed, weight_in[level])
    branch = lax.dot_general(
        act, weight_out[level], (((1,), (1,)), ((), ())), preferred_element_type=jnp.float32
    )
    saved = [(scale, normal, normed, pre, act)]
    state = (wide + branch).astype(jnp.bfloat16)
    upstream = cotangent[0]
    grads_in = [None] * level_count
    grads_out = [None] * level_count
    for level in reversed(range(level_count)):
        scale, normal, normed, pre, act = saved[level]
        grads_out[level] = lax.dot_general(
            upstream, act, (((0,), (0,)), ((), ())), preferred_element_type=jnp.float32
        ).astype(jnp.bfloat16)
        pregrad = hidden_backward(upstream, weight_out[level], pre)
        grads_in[level] = lax.dot_general(
            normed, pregrad, (((0,), (0,)), ((), ())), preferred_element_type=jnp.float32
        ).astype(jnp.bfloat16)
    return (state[None], jnp.stack(grads_in)[None], jnp.stack(grads_out)[None])


MESH = pl.DeviceIdType.MESH
F32 = jnp.float32
BF16 = jnp.bfloat16
TILE = 256


def step_order(count):
    half = count // 2
    far, near = list(range(half, count)), list(range(1, half))
    order = []
    while far or near:
        order += far[:1] + near[:1]
        far, near = far[1:], near[1:]
    return order


def partner(me, step, count):
    if count & (count - 1):
        return lax.rem(me + step, count)
    other, bit = 0, 1
    while bit < count:
        other = other + bit * lax.rem(me // bit + (step // bit) % 2, 2)
        bit *= 2
    return other


def fused_kernel(
    dims,
    pm_ref,
    tok_hbm,
    cot_hbm,
    path_in,
    path_out,
    outer_in,
    outer_out,
    moment_in,
    moment_out,
    block_hbm,
    act_hbm,
    pregrad_hbm,
    normed_t_hbm,
    cot_t_hbm,
    arr_in,
    arr_out,
    outer_v,
    moment_v,
    fresh,
    pick_in,
    pick_out,
    w_in,
    w_out,
    tok,
    cot,
    normed,
    norm_mine,
    norm_other,
    pre_mine,
    pre_other,
    slope_mine,
    slope_sent,
    slope_other,
    act,
    pregrad,
    normed_t,
    cot_t,
    state_v,
    member,
    count,
    send_sems,
    recv_sems,
    own_sems,
    pair_send,
    pair_recv,
    load_sems,
    out_sems,
):
    paths, modules, rows, owner, hidden, tokens, width = dims
    me = lax.axis_index("path")
    core = lax.axis_index("mod")
    steps = step_order(paths)
    tiles = hidden // TILE

    barrier = pltpu.get_barrier_semaphore()
    for step in steps:
        pl.semaphore_signal(
            barrier, inc=1, device_id=(partner(me, step, paths), core), device_id_type=MESH
        )
    pl.semaphore_signal(barrier, inc=1, device_id=(me, 1 - core), device_id_type=MESH)
    pl.semaphore_wait(barrier, paths)

    def span(index):
        return pl.ds(pl.multiple_of(index * owner, 16), owner)

    def gather_copy(kind, step, whole, arrived):
        dest = partner(me, step, paths)
        return pltpu.make_async_remote_copy(
            src_ref=whole.at[span(dest)],
            dst_ref=arrived.at[me],
            send_sem=send_sems.at[kind, step],
            recv_sem=recv_sems.at[kind, step],
            device_id=(dest, core),
            device_id_type=MESH,
        )

    def spread_copy(kind, step, picked, weight):
        dest = partner(me, step, paths)
        return pltpu.make_async_remote_copy(
            src_ref=picked.at[dest],
            dst_ref=weight.at[span(me)],
            send_sem=send_sems.at[kind, step],
            recv_sem=recv_sems.at[kind, step],
            device_id=(dest, core),
            device_id_type=MESH,
        )

    def pair_copy(slot, source, target):
        return pltpu.make_async_remote_copy(
            src_ref=source,
            dst_ref=target,
            send_sem=pair_send.at[slot],
            recv_sem=pair_recv.at[slot],
            device_id=(me, 1 - core),
            device_id_type=MESH,
        )

    for step in steps:
        gather_copy(0, step, path_in, arr_in).start()
    for step in steps:
        gather_copy(1, step, path_out, arr_out).start()

    own_in = pltpu.make_async_copy(path_in.at[span(me)], arr_in.at[me], own_sems.at[0])
    own_out = pltpu.make_async_copy(path_out.at[span(me)], arr_out.at[me], own_sems.at[1])
    load_tok = pltpu.make_async_copy(tok_hbm, tok, load_sems.at[0])
    load_cot = pltpu.make_async_copy(cot_hbm, cot, load_sems.at[1])
    load_outer = pltpu.make_async_copy(outer_in, outer_v, load_sems.at[2])
    load_moment = pltpu.make_async_copy(moment_in, moment_v, load_sems.at[3])
    for copy in (load_tok, load_cot, own_in, own_out, load_outer, load_moment):
        copy.start()

    for k in range(modules):
        total = jnp.float32(0.0)
        for p in range(paths):
            flag = jnp.where(pm_ref[p, 0] == k, jnp.float32(1.0), jnp.float32(0.0))
            member[k * paths + p] = flag
            total = total + flag
        count[k] = total

    load_tok.wait()
    block = 32

    @pl.loop(0, tokens // block)
    def _(i):
        at = pl.ds(pl.multiple_of(i * block, block), block)
        wide = tok[at, :].astype(F32)
        norm_mine[at, :] = jnp.broadcast_to(
            jnp.sum(wide * wide, axis=1, keepdims=True), (block, 128)
        )

    pair = pair_copy(0, norm_mine, norm_other)
    pair.start()
    pair.wait()

    @pl.loop(0, tokens // block)
    def _(i):
        at = pl.ds(pl.multiple_of(i * block, block), block)
        total = norm_mine[at, :][:, :1] + norm_other[at, :][:, :1]
        scale = lax.rsqrt(total / width + epsilon)
        normed[at, :] = (tok[at, :].astype(F32) * scale).astype(BF16)

    load_cot.wait()

    @pl.loop(0, rows // TILE)
    def _(j):
        col = pl.ds(pl.multiple_of(j * TILE, TILE), TILE)
        normed_t[col, :] = normed[:, col].astype(F32).T.astype(BF16)
        cot_t[col, :] = cot[:, col].astype(F32).T.astype(BF16)

    stores = [
        pltpu.make_async_copy(normed_t, normed_t_hbm, out_sems.at[0]),
        pltpu.make_async_copy(cot_t, cot_t_hbm, out_sems.at[1]),
    ]
    for store in stores:
        store.start()

    def update(arrived):
        columns = hidden // TILE

        @pl.loop(0, (owner // 16) * columns)
        def _(i):
            at = pl.ds(pl.multiple_of((i // columns) * 16, 16), 16)
            col = pl.ds(pl.multiple_of((i % columns) * TILE, TILE), TILE)
            sums = [jnp.zeros((16, TILE), F32) for _ in range(modules)]
            for p in range(paths):
                x = arrived[p, at, col].astype(F32)
                for k in range(modules):
                    sums[k] = sums[k] + member[k * paths + p] * x
            for k in range(modules):
                average = sums[k] / count[k]
                fresh[k, at, col] = outer_step(
                    outer_v[k, at, col], moment_v[k, at, col], average
                )

    def spread(kind, picked, weight):
        for step in steps:
            dest = partner(me, step, paths)
            picked[dest] = fresh[pm_ref[dest, 0]]
            spread_copy(kind, step, picked, weight).start()
        weight[span(me), :] = fresh[pm_ref[me, 0]]

    own_in.wait()
    load_outer.wait()
    load_moment.wait()
    for step in steps:
        gather_copy(0, step, path_in, arr_in).wait_recv()
    update(arr_in)
    load_outer = pltpu.make_async_copy(outer_out, outer_v, load_sems.at[2])
    load_moment = pltpu.make_async_copy(moment_out, moment_v, load_sems.at[3])
    load_outer.start()
    load_moment.start()
    spread(2, pick_in, w_in)

    own_out.wait()
    load_outer.wait()
    load_moment.wait()
    for step in steps:
        gather_copy(1, step, path_out, arr_out).wait_recv()
    update(arr_out)
    spread(3, pick_out, w_out)

    for step in steps:
        spread_copy(2, step, pick_in, w_in).wait_recv()

    @pl.loop(0, tiles)
    def _(j):
        col = pl.ds(pl.multiple_of(j * TILE, TILE), TILE)
        pre_mine[j] = jnp.dot(normed[...], w_in[:, col], preferred_element_type=F32)

    pair = pair_copy(1, pre_mine, pre_other)
    pair.start()
    pair.wait()

    for j in range(tiles):

        @pl.loop(0, tokens // block)
        def _(i):
            at = pl.ds(pl.multiple_of(i * block, block), block)
            pre = pre_mine[j, at, :] + pre_other[j, at, :]
            sigmoid = jax.nn.sigmoid(pre)
            act[at, j * TILE : (j + 1) * TILE] = (pre * sigmoid).astype(BF16)
            pre_mine[j, at, :] = sigmoid * (1.0 + pre * (1.0 - sigmoid))

    stores.append(pltpu.make_async_copy(act, act_hbm, out_sems.at[2]))
    stores[-1].start()

    for step in steps:
        spread_copy(3, step, pick_out, w_out).wait_recv()

    pairs = []
    for j in range(tiles):
        slope_mine[j] = jnp.dot(
            cot[...], w_out[:, j * TILE : (j + 1) * TILE], preferred_element_type=F32
        )
        slope_sent[j] = slope_mine[j].astype(BF16)
        pairs.append(pair_copy(2 + j, slope_sent.at[j], slope_other.at[j]))
        pairs[-1].start()

    @pl.loop(0, rows // TILE)
    def _(j):
        col = pl.ds(pl.multiple_of(j * TILE, TILE), TILE)
        branch = lax.dot_general(
            act[...], w_out[col, :], (((1,), (1,)), ((), ())), preferred_element_type=F32
        )
        state_v[:, col] = (tok[:, col].astype(F32) + branch).astype(BF16)

    stores.append(pltpu.make_async_copy(state_v, block_hbm, out_sems.at[3]))
    stores[-1].start()

    for j in range(tiles):
        col = slice(j * TILE, (j + 1) * TILE)
        pairs[j].wait()
        slope = slope_mine[j] + slope_other[j].astype(F32)
        pregrad[:, col] = (slope * pre_mine[j]).astype(BF16)

    stores.append(pltpu.make_async_copy(pregrad, pregrad_hbm, out_sems.at[4]))
    stores[-1].start()

    for step in steps:
        gather_copy(0, step, path_in, arr_in).wait_send()
        gather_copy(1, step, path_out, arr_out).wait_send()
        spread_copy(2, step, pick_in, w_in).wait_send()
        spread_copy(3, step, pick_out, w_out).wait_send()
    for store in stores:
        store.wait()


def finish_kernel(state, act, pregrad, normed_t, cot_t, block_out, grad_in, grad_out):
    block_out[...] = state[...]
    grad_in[...] = jnp.dot(normed_t[...], pregrad[...], preferred_element_type=F32).astype(BF16)
    grad_out[...] = jnp.dot(cot_t[...], act[...], preferred_element_type=F32).astype(BF16)


def finish(state, act, pregrad, normed_t, cot_t):
    count, rows = state.shape
    hidden = act.shape[1]
    steps = 2
    tile = rows // steps

    def split(height, length):
        return pl.BlockSpec((height, length), lambda i: (i, 0))

    def whole(height, length):
        return pl.BlockSpec((height, length), lambda i: (0, 0))

    state_spec = pl.BlockSpec((count, tile), lambda i: (0, i))
    return pl.pallas_call(
        finish_kernel,
        grid=(steps,),
        out_shape=(
            jax.ShapeDtypeStruct((count, rows), BF16),
            jax.ShapeDtypeStruct((rows, hidden), BF16),
            jax.ShapeDtypeStruct((rows, hidden), BF16),
        ),
        in_specs=[
            state_spec,
            whole(count, hidden),
            whole(count, hidden),
            split(tile, count),
            split(tile, count),
        ],
        out_specs=(state_spec, split(tile, hidden), split(tile, hidden)),
        compiler_params=pltpu.CompilerParams(vmem_limit_bytes=62 * 1024 * 1024),
        cost_estimate=pl.CostEstimate(
            flops=4 * count * rows * hidden,
            bytes_accessed=4 * rows * hidden + 8 * count * rows + 4 * count * hidden,
            transcendentals=0,
        ),
    )(state, act, pregrad, normed_t, cot_t)


def fused(
    tokens, cotangent, path_modules, path_in, path_out, outer_in, outer_out, moment_in, moment_out
):
    paths = lax.axis_size("path")
    mods = lax.axis_size("mod")
    rows, hidden = path_in.shape[2:]
    modules, owner = outer_in.shape[1:3]
    count = tokens.shape[1]
    tiles = hidden // TILE
    dims = (paths, modules, rows, owner, hidden, count, rows * mods)
    any_space = pl.BlockSpec(memory_space=pl.ANY)
    vmem = pltpu.VMEM
    out = pl.pallas_call(
        functools.partial(fused_kernel, dims),
        out_shape=(
            jax.ShapeDtypeStruct((count, rows), BF16),
            jax.ShapeDtypeStruct((count, hidden), BF16),
            jax.ShapeDtypeStruct((count, hidden), BF16),
            jax.ShapeDtypeStruct((rows, count), BF16),
            jax.ShapeDtypeStruct((rows, count), BF16),
        ),
        in_specs=[pl.BlockSpec(memory_space=pltpu.SMEM)] + [any_space] * 8,
        out_specs=(any_space,) * 5,
        scratch_shapes=[
            vmem((paths, owner, hidden), BF16),
            vmem((paths, owner, hidden), BF16),
            vmem((modules, owner, hidden), F32),
            vmem((modules, owner, hidden), F32),
            vmem((modules, owner, hidden), BF16),
            vmem((paths, owner, hidden), BF16),
            vmem((paths, owner, hidden), BF16),
            vmem((rows, hidden), BF16),
            vmem((rows, hidden), BF16),
            vmem((count, rows), BF16),
            vmem((count, rows), BF16),
            vmem((count, rows), BF16),
            vmem((count, 128), F32),
            vmem((count, 128), F32),
            vmem((tiles, count, TILE), F32),
            vmem((tiles, count, TILE), F32),
            vmem((tiles, count, TILE), F32),
            vmem((tiles, count, TILE), BF16),
            vmem((tiles, count, TILE), BF16),
            vmem((count, hidden), BF16),
            vmem((count, hidden), BF16),
            vmem((rows, count), BF16),
            vmem((rows, count), BF16),
            vmem((count, rows), BF16),
            pltpu.SMEM((modules * paths,), F32),
            pltpu.SMEM((modules,), F32),
            pltpu.SemaphoreType.DMA((4, paths)),
            pltpu.SemaphoreType.DMA((4, paths)),
            pltpu.SemaphoreType.DMA((2,)),
            pltpu.SemaphoreType.DMA((2 + tiles,)),
            pltpu.SemaphoreType.DMA((2 + tiles,)),
            pltpu.SemaphoreType.DMA((4,)),
            pltpu.SemaphoreType.DMA((5,)),
        ],
        compiler_params=pltpu.CompilerParams(
            collective_id=0, has_side_effects=True, vmem_limit_bytes=62 * 1024 * 1024
        ),
        cost_estimate=pl.CostEstimate(
            flops=10 * count * rows * hidden,
            bytes_accessed=8 * rows * hidden * 2,
            transcendentals=count * hidden,
        ),
    )(
        path_modules,
        tokens[0],
        cotangent[0],
        path_in[0, 0],
        path_out[0, 0],
        outer_in[0],
        outer_out[0],
        moment_in[0],
        moment_out[0],
    )
    state, grad_in, grad_out = finish(*out)
    return (state[None], grad_in[None, None], grad_out[None, None])


def device_program(*arrays):
    level_count, rows, hidden = arrays[3].shape[1:]
    owner = arrays[5].shape[2]
    fits = (
        level_count == 1
        and lax.axis_size("mod") == 2
        and owner % 16 == 0
        and rows % (2 * TILE) == 0
        and hidden % TILE == 0
        and arrays[0].shape[1] % 32 == 0
    )
    return fused(*arrays) if fits else local(*arrays)


def solution(mesh):
    return jax.shard_map(
        device_program,
        mesh=mesh,
        in_specs=(
            P("path", None, "mod"),
            P("path", None, "mod"),
            P(),
            P("path", None, "mod", None),
            P("path", None, "mod", None),
            P(None, None, ("mod", "path"), None),
            P(None, None, ("mod", "path"), None),
            P(None, None, ("mod", "path"), None),
            P(None, None, ("mod", "path"), None),
        ),
        out_specs=(
            P("path", None, "mod"),
            P("path", None, "mod", None),
            P("path", None, "mod", None),
        ),
        check_vma=False,
    )
```
